128 devices in a mesh: ctx: 64 (over y, z_hi, x, core), kvh: 2 (over z_lo).
Axes of the slice: x: 4, y: 4, z: 4 (z_hi: 2, z_lo: 2; z = z_hi * 2 + z_lo), core: 2. Of those that a mesh axis runs over, the one named last changes fastest.
Arguments:
- queries: bfloat16 [16384, 8192], P('ctx', 'kvh'), may hold values from -180 to 180
- keys: bfloat16 [16384, 1024], P('ctx', 'kvh'), may hold values from -6 to 6
- values: bfloat16 [16384, 1024], P('ctx', 'kvh'), may hold values from -6 to 6
- fwd_out: bfloat16 [16384, 8192], P('ctx', 'kvh'), may hold values from -4 to 4
- log_sum: float32 [64, 16384], P('kvh', 'ctx'), as said below
- out_grad: bfloat16 [16384, 8192], P('ctx', 'kvh'), may hold values from -6 to 6
- seg_ids: int32 [16384], replicated, may hold values from 0 to 15, as said below
- active: int32 [128, 16], P('ctx'), may hold values from 0 to 1, as said below
Outputs:
- grad_queries: bfloat16 [16384, 8192], P('ctx', 'kvh')
- grad_keys: bfloat16 [16384, 1024], P('ctx', 'kvh')
- grad_values: bfloat16 [16384, 1024], P('ctx', 'kvh')
The draws below stay inside these ranges and needn't reach their ends.
Inputs may be any that keep to these rules, and one draw needn't show every extreme that they name: log_sum[h, t] is the logarithm of the sum over allowed u of exp(scores[h, t, u]) for the given queries and keys. `seg_ids`: document ids never fall along the sequence; every document has 1 to 2048 tokens, and one has exactly 2048. `active`: column 0 is 1 in every row; a row has 1 to 12 ones, and the last row exactly 12.
All inputs are finite; a program needn't handle non-finite values.
Results may differ from the reference program's by a relative error of at most 0.0049.
Values may be sent and summed in bfloat16 or wider, within the bound.
A program may use at most 64 MiB of HBM per device.

```python
import jax
import jax.numpy as jnp
from jax import lax

D_HEAD = 128
QHEADS = 64
KVHEADS = 8
TOK_DEV = 256
BLK = 128
WINBLK = 16
KMAX = 12
TOKENS = 16384
NBLK = 128
N_CTX = 64


def shared_keys(key):
    base = jax.random.truncated_normal(jax.random.fold_in(key, 11), -6.0, 6.0, (TOKENS, KVHEADS * D_HEAD), jnp.float32)
    return base.astype(jnp.float32)


def shared_queries(key):
    base = jax.random.truncated_normal(jax.random.fold_in(key, 23), -6.0, 6.0, (TOKENS, QHEADS * D_HEAD), jnp.float32)
    return base.astype(jnp.float32)


def shared_segments(key):
    count = N_CTX // 4
    spread = 2 * TOK_DEV
    index = jnp.arange(count + 1, dtype=jnp.int32)
    offsets = jax.random.randint(jax.random.fold_in(key, 41), (count + 1,), 1 - spread, spread, dtype=jnp.int32)
    picked = jax.random.randint(jax.random.fold_in(key, 43), (), 1, count - 1, dtype=jnp.int32)
    phase = jax.random.randint(jax.random.fold_in(key, 47), (), 1 - spread, spread, dtype=jnp.int32)
    offsets = jnp.where(index == picked, -spread, offsets)
    offsets = jnp.where(index == picked + 1, spread, offsets)
    offsets = (offsets + phase).astype(jnp.int32)
    offsets = jnp.where((index == 0) | (index == count), 0, offsets)
    bounds = (4 * TOK_DEV * index + offsets).astype(jnp.int32)
    position = jnp.arange(TOKENS, dtype=jnp.int32)
    return jnp.sum((position[:, None] >= bounds[None, 1:count]).astype(jnp.int32), axis=1).astype(jnp.int32)


def shared_active(key):
    counts = jax.random.randint(jax.random.fold_in(key, 5), (NBLK,), 1, KMAX + 1, dtype=jnp.int32)
    counts = counts.at[NBLK - 1].set(KMAX)
    row_keys = jax.random.split(jax.random.fold_in(key, 7), NBLK)
    ranking = jax.vmap(lambda row_key: jax.random.permutation(row_key, WINBLK - 1))(row_keys).astype(jnp.int32)
    chosen = (ranking < (counts - 1)[:, None]).astype(jnp.int32)
    return jnp.concatenate([jnp.ones((NBLK, 1), jnp.int32), chosen], axis=1).astype(jnp.int32)


def draw_keys(key, part):
    return shared_keys(key).astype(jnp.bfloat16)


def draw_queries(key, part):
    return shared_queries(key).astype(jnp.bfloat16)


def draw_seg_ids(key, part):
    return shared_segments(key).astype(jnp.int32)


def draw_active(key, part):
    return shared_active(key).astype(jnp.int32)


def draw_log_sum(key, part):
    per_group = QHEADS // KVHEADS
    factor = D_HEAD ** (-0.5)
    padding = WINBLK * BLK
    query_all = shared_queries(key).astype(jnp.bfloat16).astype(jnp.float32)
    key_all = shared_keys(key).astype(jnp.bfloat16).astype(jnp.float32)
    seg_all = shared_segments(key)
    flags_all = shared_active(key)
    key_pad = jnp.pad(key_all, ((padding, 0), (0, 0)))
    seg_pad = jnp.pad(seg_all, (padding, 0), constant_values=-1)
    within = jnp.arange(BLK, dtype=jnp.int32)
    distance = jnp.arange(WINBLK, dtype=jnp.int32)

    def one_block(query_index):
        key_block = (query_index - distance).astype(jnp.int32)
        usable = jnp.repeat((flags_all[query_index] > 0) & (key_block >= 0), BLK)
        key_rows = ((key_block[:, None] * BLK + within[None, :]).reshape(-1) + padding).astype(jnp.int32)
        key_pos = key_rows - padding
        first_row = (query_index * BLK).astype(jnp.int32)
        query_pos = first_row + within
        query_seg = lax.dynamic_slice_in_dim(seg_all, first_row, BLK, 0)
        allowed = (key_pos[None, :] <= query_pos[:, None]) & (seg_pad[key_rows][None, :] == query_seg[:, None]) & usable[None, :]
        key_heads = key_pad[key_rows].reshape(WINBLK * BLK, KVHEADS, D_HEAD)
        query_heads = lax.dynamic_slice_in_dim(query_all, first_row, BLK, 0).reshape(BLK, KVHEADS, per_group, D_HEAD)
        scores = jnp.einsum('tgjd,ugd->gjtu', query_heads, key_heads) * factor
        row_max = jnp.max(jnp.where(allowed, scores, -1e+30), axis=-1, keepdims=True)
        row_sum = jnp.sum(jnp.exp(jnp.where(allowed, scores - row_max, -1e+30)), axis=-1, keepdims=True)
        return (row_max + jnp.log(row_sum))[..., 0].reshape(QHEADS, BLK)
    blocks_out = lax.map(one_block, jnp.arange(NBLK, dtype=jnp.int32))
    return jnp.transpose(blocks_out, (1, 0, 2)).reshape(QHEADS, TOKENS).astype(jnp.float32)


def block_scale(key, dims, shards, smallest, top_value):
    loudness, own = 1.0, jax.random.fold_in(key, 6)
    for axis_at, shards_of in shards:
        steps = jnp.exp(jax.random.uniform(jax.random.fold_in(own, axis_at), (shards_of,), jnp.float32, smallest / len(shards), top_value / len(shards)))
        loudness = loudness * jnp.repeat(steps, dims[axis_at] // shards_of).reshape([-1 if axis == axis_at else 1 for axis in range(len(dims))])
    return loudness


def scatter_about(stream_key, shape, scale, most, cuts=(), kind=jnp.bfloat16):
    array = scale * jax.random.normal(stream_key, shape, jnp.float32)
    if cuts:
        array = array * block_scale(stream_key, shape, cuts, -0.22, 0.18)
    return jnp.clip(array, -most, most).astype(kind)


def setup_inputs(seed: int = 0) -> dict:
    streams_of = jax.random.split(jax.random.key(seed), 9)
    queries = draw_queries(jax.random.fold_in(streams_of[8], 71), 0)
    keys = draw_keys(jax.random.fold_in(streams_of[8], 71), 0)
    values = scatter_about(streams_of[2], (TOKENS, KVHEADS * D_HEAD), 1.0, 6.0, ((0, 64), (1, 2)))
    fwd_out = scatter_about(streams_of[3], (TOKENS, QHEADS * D_HEAD), 0.5, 4.0, ((0, 64), (1, 2)))
    log_sum = draw_log_sum(jax.random.fold_in(streams_of[8], 71), 0)
    out_grad = scatter_about(streams_of[5], (TOKENS, QHEADS * D_HEAD), 1.0, 6.0, ((0, 64), (1, 2)))
    seg_ids = draw_seg_ids(jax.random.fold_in(streams_of[8], 71), 0)
    active = draw_active(jax.random.fold_in(streams_of[8], 71), 0)
    return {"queries": queries, "keys": keys, "values": values, "fwd_out": fwd_out, "log_sum": log_sum, "out_grad": out_grad, "seg_ids": seg_ids, "active": active}


LOWEST = -1.0e30


def reference(queries, keys, values, fwd_out, log_sum, out_grad, seg_ids, active):
    per_group = QHEADS // KVHEADS
    factor = D_HEAD ** -0.5
    padding = WINBLK * BLK
    window = KMAX * BLK
    key_pad = jnp.pad(keys, ((padding, 0), (0, 0)))
    value_pad = jnp.pad(values, ((padding, 0), (0, 0)))
    seg_pad = jnp.pad(seg_ids, (padding, 0), constant_values=-1)
    within = jnp.arange(BLK, dtype=jnp.int32)

    def one_block(totals, query_index):
        key_total, value_total = totals
        flags = active[query_index]
        chosen = jnp.argsort(1 - flags, stable=True)[:KMAX].astype(jnp.int32)
        in_use = flags[chosen] > 0
        key_block = (query_index - chosen).astype(jnp.int32)
        key_rows = (key_block[:, None] * BLK + within[None, :]).reshape(-1).astype(jnp.int32) + padding
        key_pos = key_rows - padding
        first_row = (query_index * BLK).astype(jnp.int32)
        query_pos = first_row + within
        query_seg = lax.dynamic_slice_in_dim(seg_ids, first_row, BLK, 0)
        usable = jnp.repeat(in_use & (key_block >= 0), BLK)
        allowed = (key_pos[None, :] <= query_pos[:, None]) & (seg_pad[key_rows][None, :] == query_seg[:, None]) & usable[None, :]
        key_heads = key_pad[key_rows].astype(jnp.float32).reshape(window, KVHEADS, D_HEAD)
        value_heads = value_pad[key_rows].astype(jnp.float32).reshape(window, KVHEADS, D_HEAD)
        query_heads = lax.dynamic_slice_in_dim(queries, first_row, BLK, 0).astype(jnp.float32).reshape(BLK, KVHEADS, per_group, D_HEAD)
        grad_heads = lax.dynamic_slice_in_dim(out_grad, first_row, BLK, 0).astype(jnp.float32).reshape(BLK, KVHEADS, per_group, D_HEAD)
        output_heads = lax.dynamic_slice_in_dim(fwd_out, first_row, BLK, 0).astype(jnp.float32).reshape(BLK, KVHEADS, per_group, D_HEAD)
        scores = jnp.einsum("tgjd,ugd->gjtu", query_heads, key_heads) * factor
        log_part = lax.dynamic_slice_in_dim(log_sum, first_row, BLK, 1).reshape(KVHEADS, per_group, BLK)[..., None]
        delta_row = jnp.einsum("tgjd,tgjd->gjt", grad_heads, output_heads)[..., None]
        weights = jnp.exp(jnp.where(allowed, scores - log_part, LOWEST))
        weights_half = lax.optimization_barrier(weights.astype(jnp.bfloat16)).astype(jnp.float32)
        grad_weights = jnp.einsum("tgjd,ugd->gjtu", grad_heads, value_heads)
        grad_scores = lax.optimization_barrier((weights * (grad_weights - delta_row)).astype(jnp.bfloat16)).astype(jnp.float32)
        grad_query = (jnp.einsum("gjtu,ugd->tgjd", grad_scores, key_heads) * factor).reshape(BLK, QHEADS * D_HEAD).astype(jnp.bfloat16)
        key_term = (jnp.einsum("gjtu,tgjd->ugd", grad_scores, query_heads) * factor).reshape(window, KVHEADS * D_HEAD)
        value_term = jnp.einsum("gjtu,tgjd->ugd", weights_half, grad_heads).reshape(window, KVHEADS * D_HEAD)
        return (key_total.at[key_rows].add(key_term), value_total.at[key_rows].add(value_term)), grad_query

    zero_sums = jnp.zeros((TOKENS + padding, KVHEADS * D_HEAD), jnp.float32)
    sums_out, grad_blocks = lax.scan(one_block, (zero_sums, zero_sums), jnp.arange(TOKENS // BLK, dtype=jnp.int32))
    grad_queries = grad_blocks.reshape(TOKENS, QHEADS * D_HEAD)
    grad_keys = sums_out[0][padding:].astype(jnp.bfloat16)
    grad_values = sums_out[1][padding:].astype(jnp.bfloat16)
    return (grad_queries, grad_keys, grad_values)
```

```python
import functools

import jax
import jax.numpy as jnp
from jax import lax
from jax.experimental import pallas as pl
from jax.experimental.pallas import tpu as pltpu
from jax.sharding import PartitionSpec as P

D = 128
BLK = 128
WIN = 16
CTX = 64
TOK = 256
CHIP = 512
HALF = 2048
NSEG = 16
FACTOR = D ** -0.5
LOG2E = 1.4426950408889634
LOWEST = -1.0e30
F32, BF16, I32 = jnp.float32, jnp.bfloat16, jnp.int32
MESH = pl.DeviceIdType.MESH
NT = (((1,), (1,)), ((), ()))
NN = (((1,), (0,)), ((), ()))
TN = (((0,), (0,)), ((), ()))


def dot(left, right, dims):
    return lax.dot_general(left, right, dims, preferred_element_type=F32)


class Place:
    def __init__(self):
        self.ctx = lax.axis_index("ctx")
        self.kvh = lax.axis_index("kvh")
        self.core = lax.rem(self.ctx, 2)
        self.chip = lax.div(self.ctx, 2)
        self.x = lax.rem(self.chip, 4)

    def sibling(self):
        return (self.ctx + 1 - 2 * self.core, self.kvh)

    def later(self, k):
        x = lax.rem(self.x + k, 4)
        return (self.ctx + 2 * (x - self.x), self.kvh)

    def line(self, step):
        return (lax.rem(self.ctx + CTX + 8 * step, CTX), self.kvh)


def enter(place):
    barrier = pltpu.get_barrier_semaphore()
    peers = [place.sibling(), place.later(1), place.later(2), place.later(3), place.line(1), place.line(-1)]
    for peer in peers:
        pl.semaphore_signal(barrier, inc=1, device_id=peer, device_id_type=MESH)
    pl.semaphore_wait(barrier, len(peers))


def remote(src, dst, send, recv, peer):
    return pltpu.make_async_remote_copy(
        src_ref=src, dst_ref=dst, send_sem=send, recv_sem=recv, device_id=peer, device_id_type=MESH
    )


def gather_kernel(q, k, v, o, lse, do, seg, act,
                  kv, qsib, dosib, rows, starts, act0, act1,
                  mine, theirs, actin, actbuf,
                  own_l, pair_s, pair_r, up_s, up_r, line_s, line_r, big_s, big_r, small_s, small_r):
    place = Place()
    core, x = place.core, place.x
    other = 1 - core
    enter(place)
    sib = place.sibling()

    def part(piece, half):
        source = (k, v)[piece % 2]
        return source.at[:, pl.ds(pl.multiple_of((half * 2 + piece // 2) * D, D), D)]

    def shelf(slot, piece):
        return kv.at[slot, piece]

    local, pair = [], []
    for p in range(4):
        dst = kv.at[4, p, pl.ds(pl.multiple_of(core * TOK, TOK), TOK), :]
        pair.append(remote(part(p, other), dst, pair_s.at[p], pair_r.at[p], sib))
        local.append(pltpu.make_async_copy(part(p, core), dst, own_l.at[p]))
        pair[p].start()
        local[p].start()
    away = pl.ds(pl.multiple_of(other * HALF, HALF), HALF)
    big = [remote(do.at[:, away], dosib, big_s.at[0], big_r.at[0], sib),
           remote(q.at[:, away], qsib, big_s.at[1], big_r.at[1], sib)]
    for copy in big:
        copy.start()
    actin[...] = jnp.zeros_like(actin)
    actin[0:2, 0:WIN] = act[...]
    small = [remote(actin, actbuf, small_s.at[0], small_r.at[0], sib)]
    small[0].start()

    up = [remote(shelf(4, p), shelf(0, p), up_s.at[p], up_r.at[p], place.line(1)) for p in range(4)]
    own_line = [[remote(shelf(4, p), shelf(4 - s, p), line_s.at[s - 1, p], line_r.at[s - 1, p], place.later(s))
                 for p in range(4)] for s in (1, 2, 3)]
    prev_line = [[remote(shelf(0, p), shelf(4 - s, p), line_s.at[s - 1, p], line_r.at[s - 1, p], place.later(s))
                  for p in range(4)] for s in (1, 2, 3)]
    for p in range(4):
        local[p].wait()
        pair[p].wait()
        up[p].start()
        for s in (1, 2, 3):
            @pl.when(x + s < 4)
            def _(s=s, p=p):
                own_line[s - 1][p].start()

    spread = jnp.where(lax.broadcasted_iota(I32, (8, 8 * D), 1) // D == lax.broadcasted_iota(I32, (8, 8 * D), 0),
                       1.0, 0.0).astype(BF16)
    for g in range(4):
        cols = slice(g * 8 * D, (g + 1) * 8 * D)
        product = do[:, cols].astype(F32) * o[:, cols].astype(F32)
        high = product.astype(BF16)
        low = (product - high.astype(F32)).astype(BF16)
        delta = dot(spread, high, NT) + dot(spread, low, NT)
        logs = lse[g * 8:(g + 1) * 8, :] * LOG2E

        @pl.when(core == g // 2)
        def _(delta=delta, logs=logs, g=g):
            mine[0, g % 2] = logs
            mine[1, g % 2] = delta

        @pl.when(core != g // 2)
        def _(delta=delta, logs=logs, g=g):
            theirs[0, g % 2] = logs
            theirs[1, g % 2] = delta

    small.append(remote(theirs, rows.at[core], small_s.at[1], small_r.at[1], sib))
    small[1].start()
    place_rows = pltpu.make_async_copy(mine, rows.at[core], own_l.at[4])

    seg_all = seg[...]
    seg_here = seg[pl.ds(place.chip * 4, 4), :]
    first = jnp.zeros((4, BLK), I32)
    for s in range(1, NSEG):
        first = jnp.where(seg_here == s, jnp.sum((seg_all < s).astype(I32)), first)
    starts[...] = jnp.zeros_like(starts)
    starts[0:4, :] = first

    for p in range(4):
        up[p].wait_recv()
        for s in (1, 2, 3):
            @pl.when(x + s >= 4)
            def _(s=s, p=p):
                prev_line[s - 1][p].start()
    for p in range(4):
        up[p].wait_send()
        for s in (1, 2, 3):
            own_line[s - 1][p].wait()
    for copy in big + small:
        copy.wait()
    place_rows.start()
    place_rows.wait()

    @pl.when(core == 0)
    def _():
        act0[...] = actin[...]
        act1[...] = actbuf[...]

    @pl.when(core == 1)
    def _():
        act0[...] = actbuf[...]
        act1[...] = actin[...]


def gather(q, k, v, o, lse, do, seg, act):
    anywhere = pl.BlockSpec(memory_space=pl.ANY)
    vmem = pl.BlockSpec(memory_space=pltpu.VMEM)
    dma = pltpu.SemaphoreType.DMA
    return pl.pallas_call(
        gather_kernel,
        out_shape=[
            jax.ShapeDtypeStruct((5, 4, CHIP, D), BF16),
            jax.ShapeDtypeStruct((TOK, HALF), BF16),
            jax.ShapeDtypeStruct((TOK, HALF), BF16),
            jax.ShapeDtypeStruct((2, 2, 2, 8, TOK), F32),
            jax.ShapeDtypeStruct((8, BLK), I32),
            jax.ShapeDtypeStruct((8, BLK), I32),
            jax.ShapeDtypeStruct((8, BLK), I32),
        ],
        in_specs=[anywhere, anywhere, anywhere, vmem, vmem, vmem, vmem, vmem],
        out_specs=[anywhere, anywhere, anywhere, anywhere, vmem, vmem, vmem],
        scratch_shapes=[
            pltpu.VMEM((2, 2, 8, TOK), F32),
            pltpu.VMEM((2, 2, 8, TOK), F32),
            pltpu.VMEM((8, BLK), I32),
            pltpu.VMEM((8, BLK), I32),
            dma((5,)), dma((4,)), dma((4,)), dma((4,)), dma((4,)), dma((3, 4)), dma((3, 4)),
            dma((2,)), dma((2,)), dma((2,)), dma((2,)),
        ],
        compiler_params=pltpu.CompilerParams(
            collective_id=0, has_side_effects=True, vmem_limit_bytes=63 * 2 ** 20),
        name="gather",
    )(q, k, v, o, lse, do, seg, act)


def compute_kernel(starts_s, act0, act1, starts_v, rows, kv, q, do, qsib, dosib,
                   parts, own, dq,
                   qv, dov, dq_sum, kv_sum, list_q, list_k, sems):
    core = lax.rem(lax.axis_index("ctx"), 2)
    chip = lax.div(lax.axis_index("ctx"), 2)
    here = pl.ds(pl.multiple_of(core * HALF, HALF), HALF)
    mine = pl.ds(pl.multiple_of(core * TOK, TOK), TOK)
    theirs = pl.ds(pl.multiple_of((1 - core) * TOK, TOK), TOK)
    loads = [
        pltpu.make_async_copy(q.at[:, here], qv.at[mine, :], sems.at[0]),
        pltpu.make_async_copy(qsib, qv.at[theirs, :], sems.at[1]),
        pltpu.make_async_copy(do.at[:, here], dov.at[mine, :], sems.at[2]),
        pltpu.make_async_copy(dosib, dov.at[theirs, :], sems.at[3]),
    ]
    for copy in loads:
        copy.start()

    count = jnp.int32(0)
    for a in range(4):
        first = starts_s[a, 0]
        flags = (act0, act1)[a // 2]

        def consider(d, count, a=a, first=first, flags=flags):
            reach = ((chip * 4 + a - d) * BLK + (BLK - 1) >= first) & (flags[a % 2, d] > 0)
            list_q[count] = a
            list_k[count] = 16 + a - d
            return count + reach.astype(I32)

        count = lax.fori_loop(0, WIN, consider, count)
    list_q[count] = 0
    list_k[count] = 16

    dq_sum[...] = jnp.zeros_like(dq_sum)
    kv_sum[...] = jnp.zeros_like(kv_sum)
    for copy in loads:
        copy.wait()

    key_at = lax.broadcasted_iota(I32, (BLK, BLK), 0)
    query_at = lax.broadcasted_iota(I32, (1, BLK), 1)

    def chain(entry):
        a, rel = list_q[entry], list_k[entry]
        slot, block = lax.div(rel, 4), lax.rem(rel, 4)
        offset = pl.multiple_of(block * BLK, BLK)
        keys = pl.ds(offset, BLK)
        tokens = pl.ds(pl.multiple_of(a * BLK, BLK), BLK)
        base = (chip * 4 - 16 + rel) * BLK
        first = jnp.where(entry < count, starts_v[pl.ds(a, 1), :], 2 ** 30) - base
        last = (chip * 4 + a) * BLK + query_at - base
        bias = jnp.where((key_at >= first) & (key_at <= last), 0.0, LOWEST)
        for g in range(2):
            key, value = kv[slot, 2 * g, keys, :], kv[slot, 2 * g + 1, keys, :]
            columns = [slice((g * 8 + j) * D, (g * 8 + j + 1) * D) for j in range(8)]
            query = jnp.concatenate([qv[tokens, c] for c in columns], 0)
            cotangent = jnp.concatenate([dov[tokens, c] for c in columns], 0)
            scores = dot(key, query, NT)
            grad_weights = dot(value, cotangent, NT)
            half = lax.div(a, 2)
            lanes = pl.ds(pl.multiple_of(lax.rem(a, 2) * BLK, BLK), BLK)
            weights, grad_scores = [], []
            for j in range(8):
                lane = slice(j * BLK, (j + 1) * BLK)
                log_row = rows[half, 0, g, j:j + 1, lanes]
                delta_row = rows[half, 1, g, j:j + 1, lanes]
                weight = jnp.exp2(scores[:, lane] * (FACTOR * LOG2E) - log_row + bias)
                weights.append(weight.astype(BF16))
                grad_scores.append((weight * (grad_weights[:, lane] - delta_row)).astype(BF16))
            weights = jnp.concatenate(weights, 1)
            grad_scores = jnp.concatenate(grad_scores, 1)
            kv_sum[slot, 2 * g, keys, :] += dot(grad_scores, query, NN)
            kv_sum[slot, 2 * g + 1, keys, :] += dot(weights, cotangent, NN)
            dq_sum[a, g] += dot(key, grad_scores, TN)

    def step(i, carry):
        chain(2 * i)
        chain(2 * i + 1)
        return carry

    lax.fori_loop(0, lax.div(count + 1, 2), step, 0)

    for p in range(4):
        scale = FACTOR if p % 2 == 0 else 1.0
        for s in range(4):
            parts[s, p] = (kv_sum[s, p] * scale).astype(BF16)
        own[p] = kv_sum[4, p] * scale

    def turn(i, carry):
        a, g = lax.div(i, 2), lax.rem(i, 2)
        tokens = pl.ds(pl.multiple_of(a * BLK, BLK), BLK)
        for j in range(8):
            block = dq_sum[a, g, :, j * BLK:(j + 1) * BLK].T * FACTOR
            dq[tokens, pl.ds(pl.multiple_of((g * 8 + j) * D, D), D)] = block.astype(BF16)
        return carry

    lax.fori_loop(0, 8, turn, 0)


def compute(starts, act0, act1, rows, kv, q, do, qsib, dosib):
    anywhere = pl.BlockSpec(memory_space=pl.ANY)
    vmem = pl.BlockSpec(memory_space=pltpu.VMEM)
    smem = pl.BlockSpec(memory_space=pltpu.SMEM)
    return pl.pallas_call(
        compute_kernel,
        out_shape=[
            jax.ShapeDtypeStruct((4, 4, CHIP, D), BF16),
            jax.ShapeDtypeStruct((4, CHIP, D), F32),
            jax.ShapeDtypeStruct((CHIP, HALF), BF16),
        ],
        in_specs=[smem, smem, smem, vmem, vmem, vmem, anywhere, anywhere, anywhere, anywhere],
        out_specs=[vmem, vmem, vmem],
        scratch_shapes=[
            pltpu.VMEM((CHIP, HALF), BF16),
            pltpu.VMEM((CHIP, HALF), BF16),
            pltpu.VMEM((4, 2, D, 8 * BLK), F32),
            pltpu.VMEM((5, 4, CHIP, D), F32),
            pltpu.SMEM((72,), I32),
            pltpu.SMEM((72,), I32),
            pltpu.SemaphoreType.DMA((4,)),
        ],
        compiler_params=pltpu.CompilerParams(vmem_limit_bytes=63 * 2 ** 20),
        name="compute",
    )(starts, act0, act1, starts, rows, kv, q, do, qsib, dosib)


def return_kernel(parts, own, dq,
                  gq, gk, gv,
                  far, got, relay, total, final,
                  load_s, line_s, line_r, up_s, up_r, out_s, fin_s, fin_r, q_s, q_r):
    place = Place()
    core, x = place.core, place.x
    other = 1 - core
    here = pl.ds(pl.multiple_of(core * HALF, HALF), HALF)
    mine = pl.ds(pl.multiple_of(core * TOK, TOK), TOK)
    theirs = pl.ds(pl.multiple_of(other * TOK, TOK), TOK)
    loads = [pltpu.make_async_copy(parts.at[0], far, load_s.at[0]),
             pltpu.make_async_copy(own, total, load_s.at[1])]
    for copy in loads:
        copy.start()
    enter(place)
    sib = place.sibling()
    line = [[remote(parts.at[4 - s, p], got.at[s - 1, p], line_s.at[s - 1, p], line_r.at[s - 1, p], place.later(4 - s))
             for p in range(4)] for s in (1, 2, 3)]
    for p in range(4):
        for s in (1, 2, 3):
            @pl.when(x - s < 0)
            def _(s=s, p=p):
                line[s - 1][p].start()
    for p in range(4):
        for s in (1, 2, 3):
            @pl.when(x - s >= 0)
            def _(s=s, p=p):
                line[s - 1][p].start()
    send_q = remote(dq.at[theirs, :], gq.at[:, here], q_s.at[0], q_r.at[0], sib)
    send_q.start()
    keep_q = pltpu.make_async_copy(dq.at[mine, :], gq.at[:, here], load_s.at[2])
    keep_q.start()
    for copy in loads:
        copy.wait()

    up = [remote(relay.at[p], got.at[3, p], up_s.at[p], up_r.at[p], place.line(-1)) for p in range(4)]
    for p in range(4):
        summed = far[p].astype(F32)
        final[...] = summed
        for s in (3, 2, 1):
            @pl.when(x + s >= 4)
            def _(s=s, p=p):
                line[s - 1][p].wait_recv()
                final[...] += got[s - 1, p].astype(F32)
        relay[p] = final[...].astype(BF16)
        up[p].start()
    finish = []
    for p in range(4):
        for s in (1, 2, 3):
            @pl.when(x + s < 4)
            def _(s=s, p=p):
                line[s - 1][p].wait_recv()
                total[p] += got[s - 1, p].astype(F32)
    for p in range(4):
        up[p].wait_recv()
        far[p] = (total[p] + got[3, p].astype(F32)).astype(BF16)
        columns = pl.ds(pl.multiple_of((core * 2 + p // 2) * D, D), D)
        target = (gk, gv)[p % 2].at[:, columns]
        finish.append(remote(far.at[p, theirs, :], target, fin_s.at[p], fin_r.at[p], sib))
        finish[p].start()
        keep = pltpu.make_async_copy(far.at[p, mine, :], target, out_s.at[p])
        keep.start()
    for p in range(4):
        pltpu.make_async_copy(
            far.at[p, mine, :],
            (gk, gv)[p % 2].at[:, pl.ds(pl.multiple_of((core * 2 + p // 2) * D, D), D)], out_s.at[p]).wait()
        finish[p].wait()
        up[p].wait_send()
        for s in (1, 2, 3):
            line[s - 1][p].wait_send()
    send_q.wait()
    keep_q.wait()


def give_back(parts, own, dq):
    anywhere = pl.BlockSpec(memory_space=pl.ANY)
    dma = pltpu.SemaphoreType.DMA
    return pl.pallas_call(
        return_kernel,
        out_shape=[
            jax.ShapeDtypeStruct((TOK, 2 * HALF), BF16),
            jax.ShapeDtypeStruct((TOK, 4 * D), BF16),
            jax.ShapeDtypeStruct((TOK, 4 * D), BF16),
        ],
        in_specs=[anywhere] * 3,
        out_specs=[anywhere] * 3,
        scratch_shapes=[
            pltpu.VMEM((4, CHIP, D), BF16),
            pltpu.VMEM((4, 4, CHIP, D), BF16),
            pltpu.VMEM((4, CHIP, D), BF16),
            pltpu.VMEM((4, CHIP, D), F32),
            pltpu.VMEM((CHIP, D), F32),
            dma((3,)), dma((3, 4)), dma((3, 4)), dma((4,)), dma((4,)), dma((4,)), dma((4,)), dma((4,)),
            dma((1,)), dma((1,)),
        ],
        compiler_params=pltpu.CompilerParams(
            collective_id=1, has_side_effects=True, vmem_limit_bytes=63 * 2 ** 20),
        name="give_back",
    )(parts, own, dq)


def body(queries, keys, values, fwd_out, log_sum, out_grad, seg_ids, active):
    seg = seg_ids.reshape(TOK // 2, BLK)
    kv, qsib, dosib, rows, starts, act0, act1 = gather(
        queries, keys, values, fwd_out, log_sum, out_grad, seg, active)
    parts, own, dq = compute(starts, act0, act1, rows, kv, queries, out_grad, qsib, dosib)
    return tuple(give_back(parts, own, dq))


def solution(mesh):
    placed = (
        P("ctx", "kvh"), P("ctx", "kvh"), P("ctx", "kvh"), P("ctx", "kvh"),
        P("kvh", "ctx"), P("ctx", "kvh"), P(), P("ctx", None),
    )
    return jax.shard_map(
        body, mesh=mesh, in_specs=placed,
        out_specs=(P("ctx", "kvh"), P("ctx", "kvh"), P("ctx", "kvh")),
        check_vma=False,
    )
```

```python
import functools

import jax
import jax.numpy as jnp
from jax import lax
from jax.experimental import pallas as pl
from jax.experimental.pallas import tpu as pltpu
from jax.sharding import PartitionSpec as P

D = 128
BLK = 128
WIN = 16
CTX = 64
TOK = 256
CHIP = 512
HALF = 2048
NSEG = 16
FACTOR = D ** -0.5
LOG2E = 1.4426950408889634
LOWEST = -1.0e30
F32, BF16, I32 = jnp.float32, jnp.bfloat16, jnp.int32
MESH = pl.DeviceIdType.MESH
NT = (((1,), (1,)), ((), ()))
NN = (((1,), (0,)), ((), ()))
TN = (((0,), (0,)), ((), ()))


def dot(left, right, dims):
    return lax.dot_general(left, right, dims, preferred_element_type=F32)


class Place:
    def __init__(self):
        self.ctx = lax.axis_index("ctx")
        self.kvh = lax.axis_index("kvh")
        self.core = lax.rem(self.ctx, 2)
        self.chip = lax.div(self.ctx, 2)
        self.x = lax.rem(self.chip, 4)

    def sibling(self):
        return (self.ctx + 1 - 2 * self.core, self.kvh)

    def later(self, k):
        x = lax.rem(self.x + k, 4)
        return (self.ctx + 2 * (x - self.x), self.kvh)

    def line(self, step):
        return (lax.rem(self.ctx + CTX + 8 * step, CTX), self.kvh)


def enter(place):
    barrier = pltpu.get_barrier_semaphore()
    peers = [place.sibling(), place.later(1), place.later(2), place.later(3), place.line(1), place.line(-1)]
    for peer in peers:
        pl.semaphore_signal(barrier, inc=1, device_id=peer, device_id_type=MESH)
    pl.semaphore_wait(barrier, len(peers))


def remote(src, dst, send, recv, peer):
    return pltpu.make_async_remote_copy(
        src_ref=src, dst_ref=dst, send_sem=send, recv_sem=recv, device_id=peer, device_id_type=MESH
    )


def fused_kernel(q, k, v, o, lse, do, seg, act,
                 gq, gk, gv,
                 kv, qv, dov, o_v, d_v, rows, theirs, actin, actbuf, firsts,
                 dq_sum, kv_sum, own_sum, parts, far, got, relay, final, dq,
                 load_s, pair_l, pair_s, pair_r, up_s, up_r, line_s, line_r, big_s, big_r, small_s, small_r,
                 back_s, back_r, down_s, down_r, out_s, fin_s, fin_r, q_s, q_r):
    place = Place()
    core, x, chip = place.core, place.x, place.chip
    other = 1 - core
    sib = place.sibling()
    here = pl.ds(pl.multiple_of(core * HALF, HALF), HALF)
    away = pl.ds(pl.multiple_of(other * HALF, HALF), HALF)
    mine = pl.ds(pl.multiple_of(core * TOK, TOK), TOK)
    others = pl.ds(pl.multiple_of(other * TOK, TOK), TOK)

    def part(piece, half):
        source = (k, v)[piece % 2]
        return source.at[:, pl.ds(pl.multiple_of((half * 2 + piece // 2) * D, D), D)]

    def shelf(slot, piece):
        return kv.at[slot, piece]

    local = [pltpu.make_async_copy(part(p, core), kv.at[4, p, mine, :], pair_l.at[p]) for p in range(4)]
    loads = [
        pltpu.make_async_copy(do, d_v, load_s.at[0]),
        pltpu.make_async_copy(o, o_v, load_s.at[1]),
        pltpu.make_async_copy(do.at[:, here], dov.at[mine, :], load_s.at[2]),
        pltpu.make_async_copy(q.at[:, here], qv.at[mine, :], load_s.at[3]),
    ]
    for copy in local + loads:
        copy.start()
    actin[...] = jnp.zeros_like(actin)
    actin[0:2, 0:WIN] = act[...]
    enter(place)

    pair = [remote(part(p, other), kv.at[4, p, mine, :], pair_s.at[p], pair_r.at[p], sib) for p in range(4)]
    big = [remote(do.at[:, away], dov.at[mine, :], big_s.at[0], big_r.at[0], sib),
           remote(q.at[:, away], qv.at[mine, :], big_s.at[1], big_r.at[1], sib)]
    small = [remote(actin, actbuf, small_s.at[0], small_r.at[0], sib),
             remote(theirs, rows.at[core], small_s.at[1], small_r.at[1], sib)]
    for copy in pair + [small[0]] + big:
        copy.start()

    up = [remote(shelf(4, p), shelf(0, p), up_s.at[p], up_r.at[p], place.line(1)) for p in range(4)]
    own_line = [[remote(shelf(4, p), shelf(4 - s, p), line_s.at[s - 1, p], line_r.at[s - 1, p], place.later(s))
                 for p in range(4)] for s in (1, 2, 3)]
    prev_line = [[remote(shelf(0, p), shelf(4 - s, p), line_s.at[s - 1, p], line_r.at[s - 1, p], place.later(s))
                  for p in range(4)] for s in (1, 2, 3)]
    for p in range(4):
        local[p].wait()
        pair[p].wait()
        up[p].start()
        for s in (1, 2, 3):
            @pl.when(x + s < 4)
            def _(s=s, p=p):
                own_line[s - 1][p].start()

    loads[0].wait()
    loads[1].wait()
    spread = jnp.where(lax.broadcasted_iota(I32, (8, 8 * D), 1) // D == lax.broadcasted_iota(I32, (8, 8 * D), 0),
                       1.0, 0.0).astype(BF16)
    for g in range(4):
        cols = slice(g * 8 * D, (g + 1) * 8 * D)
        product = d_v[:, cols].astype(F32) * o_v[:, cols].astype(F32)
        high = product.astype(BF16)
        low = (product - high.astype(F32)).astype(BF16)
        delta = dot(spread, high, NT) + dot(spread, low, NT)
        logs = lse[g * 8:(g + 1) * 8, :] * LOG2E

        @pl.when(core == g // 2)
        def _(delta=delta, logs=logs, g=g):
            rows[core, 0, g % 2] = logs
            rows[core, 1, g % 2] = delta

        @pl.when(core != g // 2)
        def _(delta=delta, logs=logs, g=g):
            theirs[0, g % 2] = logs
            theirs[1, g % 2] = delta

    small[1].start()

    seg_all = seg[...]
    seg_here = seg[pl.ds(chip * 4, 4), :]
    first = jnp.zeros((4, BLK), I32)
    for s in range(1, NSEG):
        first = jnp.where(seg_here == s, jnp.sum((seg_all < s).astype(I32)), first)
    small[0].wait()
    flags = [jnp.where(core == 0, actin[...], actbuf[...]), jnp.where(core == 0, actbuf[...], actin[...])]
    firsts[...] = jnp.full(firsts.shape, 2 ** 30, I32)
    for a in range(4):
        for d in range(WIN):
            flag = jnp.broadcast_to(flags[a // 2][a % 2:a % 2 + 1, d:d + 1], (1, BLK))
            firsts[a, d:d + 1, :] = jnp.where(flag > 0, first[a:a + 1, :], 2 ** 30)
    dq_sum[...] = jnp.zeros_like(dq_sum)

    key_at = lax.broadcasted_iota(I32, (BLK, BLK), 0)
    query_at = lax.broadcasted_iota(I32, (1, BLK), 1)

    def tile(slot, a, h):
        keys = pl.ds(pl.multiple_of(h * 2 * BLK, 2 * BLK), 2 * BLK)
        tokens = pl.ds(pl.multiple_of(a * BLK, BLK), BLK)
        lanes = pl.ds(pl.multiple_of(lax.rem(a, 2) * BLK, BLK), BLK)
        half = lax.div(a, 2)
        bias = []
        for b in range(2):
            rel = slot * 4 + h * 2 + b
            base = (chip * 4 - 16 + rel) * BLK
            low = firsts[a, pl.ds(jnp.maximum(16 + a - rel, 0), 1), :] - base
            high = (chip * 4 + a) * BLK - base + query_at
            bias.append(jnp.where((key_at >= low) & (key_at <= high), 0.0, LOWEST))
        bias = jnp.concatenate(bias, 0)
        for g in range(2):
            key, value = kv[slot, 2 * g, keys, :], kv[slot, 2 * g + 1, keys, :]
            columns = [slice((g * 8 + j) * D, (g * 8 + j + 1) * D) for j in range(8)]
            query = jnp.concatenate([qv[tokens, c] for c in columns], 0)
            cotangent = jnp.concatenate([dov[tokens, c] for c in columns], 0)
            scores = dot(key, query, NT)
            grad_weights = dot(value, cotangent, NT)
            weights, grad_scores = [], []
            for j in range(8):
                lane = slice(j * BLK, (j + 1) * BLK)
                log_row = rows[half, 0, g, j:j + 1, lanes]
                delta_row = rows[half, 1, g, j:j + 1, lanes]
                weight = jnp.exp2(scores[:, lane] * (FACTOR * LOG2E) - log_row + bias)
                weights.append(weight.astype(BF16))
                grad_scores.append((weight * (grad_weights[:, lane] - delta_row)).astype(BF16))
            weights = jnp.concatenate(weights, 1)
            grad_scores = jnp.concatenate(grad_scores, 1)
            kv_sum[2 * g, keys, :] += dot(grad_scores, query, NN)
            kv_sum[2 * g + 1, keys, :] += dot(weights, cotangent, NN)
            dq_sum[a, g] += dot(key, grad_scores, TN)

    def phase(slot, steps, pairs, after=None):
        kv_sum[...] = jnp.zeros_like(kv_sum)

        def step(i, carry):
            for a, h in pairs(i):
                tile(slot, a, h)
            if after is not None:
                after(i)
            return carry

        lax.fori_loop(0, steps, step, 0)

    back = [[remote(parts.at[s - 1, p], got.at[s - 1, p], back_s.at[s - 1, p], back_r.at[s - 1, p], place.later(4 - s))
             for p in range(4)] for s in (1, 2, 3)]

    def full_phase(s):
        for p in range(4):
            prev_line[s - 1][p].wait_recv()
        phase(4 - s, 4, lambda i: [(i, 0), (i, 1)])
        for p in range(4):
            parts[s - 1, p] = (kv_sum[p] * (FACTOR if p % 2 == 0 else 1.0)).astype(BF16)
            back[s - 1][p].start()

    def forward(p):
        remote(shelf(4, p), shelf(0, p), up_s.at[p], up_r.at[p], place.line(1)).wait_recv()
        for s in (1, 3, 2):
            @pl.when(x + s >= 4)
            def _(s=s):
                remote(shelf(0, p), shelf(4 - s, p), line_s.at[s - 1, p], line_r.at[s - 1, p], place.later(s)).start()

    for copy in loads[2:] + big + [small[1]]:
        copy.wait()
    forward(0)
    phase(4, 3, lambda i: [(jnp.where(i == 0, 0, i + 1), 0), (i + 1, jnp.where(i == 0, 0, 1))],
          lambda i: forward(i + 1))
    for p in range(4):
        own_sum[p] = kv_sum[p] * (FACTOR if p % 2 == 0 else 1.0)
    full_phase(1)
    full_phase(3)
    full_phase(2)
    phase(0, 2, lambda i: [(i, i), (2 * i, 1)])
    for p in range(4):
        far[p] = (kv_sum[p] * (FACTOR if p % 2 == 0 else 1.0)).astype(BF16)

    def turn(i, carry):
        a, g = lax.div(i, 2), lax.rem(i, 2)
        tokens = pl.ds(pl.multiple_of(a * BLK, BLK), BLK)
        for j in range(8):
            block = dq_sum[a, g, :, j * BLK:(j + 1) * BLK].T * FACTOR
            dq[tokens, pl.ds(pl.multiple_of((g * 8 + j) * D, D), D)] = block.astype(BF16)
        return carry

    lax.fori_loop(0, 8, turn, 0)
    send_q = remote(dq.at[others, :], gq.at[:, here], q_s.at[0], q_r.at[0], sib)
    send_q.start()
    keep_q = pltpu.make_async_copy(dq.at[mine, :], gq.at[:, here], load_s.at[4])
    keep_q.start()

    down = [remote(relay.at[p], got.at[3, p], down_s.at[p], down_r.at[p], place.line(-1)) for p in range(4)]
    for p in range(4):
        final[...] = far[p].astype(F32)
        for s in (3, 2, 1):
            @pl.when(x + s >= 4)
            def _(s=s, p=p):
                back[s - 1][p].wait_recv()
                final[...] += got[s - 1, p].astype(F32)
        relay[p] = final[...].astype(BF16)
        down[p].start()
    for p in range(4):
        for s in (1, 3, 2):
            @pl.when(x + s < 4)
            def _(s=s, p=p):
                back[s - 1][p].wait_recv()
                own_sum[p] += got[s - 1, p].astype(F32)
    finish, keep = [], []
    for p in range(4):
        down[p].wait_recv()
        far[p] = (own_sum[p] + got[3, p].astype(F32)).astype(BF16)
        target = (gk, gv)[p % 2].at[:, pl.ds(pl.multiple_of((core * 2 + p // 2) * D, D), D)]
        finish.append(remote(far.at[p, others, :], target, fin_s.at[p], fin_r.at[p], sib))
        keep.append(pltpu.make_async_copy(far.at[p, mine, :], target, out_s.at[p]))
        finish[p].start()
        keep[p].start()
    for p in range(4):
        keep[p].wait()
        finish[p].wait()
        up[p].wait_send()
        down[p].wait_send()
        for s in (1, 2, 3):
            prev_line[s - 1][p].wait_send()
            back[s - 1][p].wait_send()
    send_q.wait()
    keep_q.wait()


def body(queries, keys, values, fwd_out, log_sum, out_grad, seg_ids, active):
    anywhere = pl.BlockSpec(memory_space=pl.ANY)
    vmem = pl.BlockSpec(memory_space=pltpu.VMEM)
    dma = pltpu.SemaphoreType.DMA
    seg = seg_ids.reshape(BLK, BLK)
    return tuple(pl.pallas_call(
        fused_kernel,
        out_shape=[
            jax.ShapeDtypeStruct((TOK, 2 * HALF), BF16),
            jax.ShapeDtypeStruct((TOK, 4 * D), BF16),
            jax.ShapeDtypeStruct((TOK, 4 * D), BF16),
        ],
        in_specs=[anywhere, anywhere, anywhere, anywhere, vmem, anywhere, vmem, vmem],
        out_specs=[anywhere] * 3,
        scratch_shapes=[
            pltpu.VMEM((5, 4, CHIP, D), BF16),
            pltpu.VMEM((CHIP, HALF), BF16),
            pltpu.VMEM((CHIP, HALF), BF16),
            pltpu.VMEM((TOK, 2 * HALF), BF16),
            pltpu.VMEM((TOK, 2 * HALF), BF16),
            pltpu.VMEM((2, 2, 2, 8, TOK), F32),
            pltpu.VMEM((2, 2, 8, TOK), F32),
            pltpu.VMEM((8, BLK), I32),
            pltpu.VMEM((8, BLK), I32),
            pltpu.VMEM((4, 24, BLK), I32),
            pltpu.VMEM((4, 2, D, 8 * BLK), F32),
            pltpu.VMEM((4, CHIP, D), F32),
            pltpu.VMEM((4, CHIP, D), F32),
            pltpu.VMEM((3, 4, CHIP, D), BF16),
            pltpu.VMEM((4, CHIP, D), BF16),
            pltpu.VMEM((4, 4, CHIP, D), BF16),
            pltpu.VMEM((4, CHIP, D), BF16),
            pltpu.VMEM((CHIP, D), F32),
            pltpu.VMEM((CHIP, HALF), BF16),
            dma((5,)), dma((4,)), dma((4,)), dma((4,)), dma((4,)), dma((4,)), dma((3, 4)), dma((3, 4)),
            dma((2,)), dma((2,)), dma((2,)), dma((2,)),
            dma((3, 4)), dma((3, 4)), dma((4,)), dma((4,)), dma((4,)), dma((4,)), dma((4,)), dma((1,)), dma((1,)),
        ],
        compiler_params=pltpu.CompilerParams(
            collective_id=0, has_side_effects=True, vmem_limit_bytes=63 * 2 ** 20),
        cost_estimate=pl.CostEstimate(flops=25 * 10 ** 9, bytes_accessed=12 * 2 ** 20, transcendentals=0),
        name="fused",
    )(queries, keys, values, fwd_out, log_sum, out_grad, seg, active))


def solution(mesh):
    placed = (
        P("ctx", "kvh"), P("ctx", "kvh"), P("ctx", "kvh"), P("ctx", "kvh"),
        P("kvh", "ctx"), P("ctx", "kvh"), P(), P("ctx", None),
    )
    return jax.shard_map(
        body, mesh=mesh, in_specs=placed,
        out_specs=(P("ctx", "kvh"), P("ctx", "kvh"), P("ctx", "kvh")),
        check_vma=False,
    )
```

```python
import functools

import jax
import jax.numpy as jnp
from jax import lax
from jax.experimental import pallas as pl
from jax.experimental.pallas import tpu as pltpu
from jax.sharding import PartitionSpec as P

D = 128
BLK = 128
WIN = 16
CTX = 64
TOK = 256
CHIP = 512
HALF = 2048
NSEG = 16
FACTOR = D ** -0.5
LOG2E = 1.4426950408889634
LOWEST = -1.0e30
F32, BF16, I32 = jnp.float32, jnp.bfloat16, jnp.int32
MESH = pl.DeviceIdType.MESH
NT = (((1,), (1,)), ((), ()))
NN = (((1,), (0,)), ((), ()))
TN = (((0,), (0,)), ((), ()))


def dot(left, right, dims):
    return lax.dot_general(left, right, dims, preferred_element_type=F32)


class Place:
    def __init__(self):
        self.ctx = lax.axis_index("ctx")
        self.kvh = lax.axis_index("kvh")
        self.core = lax.rem(self.ctx, 2)
        self.chip = lax.div(self.ctx, 2)
        self.x = lax.rem(self.chip, 4)

    def sibling(self):
        return (self.ctx + 1 - 2 * self.core, self.kvh)

    def later(self, k):
        x = lax.rem(self.x + k, 4)
        return (self.ctx + 2 * (x - self.x), self.kvh)

    def line(self, step):
        return (lax.rem(self.ctx + CTX + 8 * step, CTX), self.kvh)


def enter(place):
    barrier = pltpu.get_barrier_semaphore()
    peers = [place.sibling(), place.later(1), place.later(2), place.later(3), place.line(1), place.line(-1)]
    for peer in peers:
        pl.semaphore_signal(barrier, inc=1, device_id=peer, device_id_type=MESH)
    pl.semaphore_wait(barrier, len(peers))


def remote(src, dst, send, recv, peer):
    return pltpu.make_async_remote_copy(
        src_ref=src, dst_ref=dst, send_sem=send, recv_sem=recv, device_id=peer, device_id_type=MESH
    )


def fused_kernel(q, k, v, o, lse, do, seg, act,
                 gq, gk, gv,
                 kv, qv, dov, o_v, d_v, rows, theirs, actin, actbuf, firsts,
                 dq_sum, kv_sum, own_sum, parts, far, got, relay, final, dq,
                 load_s, pair_l, pair_s, pair_r, up_s, up_r, line_s, line_r, big_s, big_r, small_s, small_r,
                 back_s, back_r, down_s, down_r, out_s, fin_s, fin_r, q_s, q_r):
    place = Place()
    core, x, chip = place.core, place.x, place.chip
    other = 1 - core
    sib = place.sibling()
    here = pl.ds(pl.multiple_of(core * HALF, HALF), HALF)
    away = pl.ds(pl.multiple_of(other * HALF, HALF), HALF)
    mine = pl.ds(pl.multiple_of(core * TOK, TOK), TOK)
    others = pl.ds(pl.multiple_of(other * TOK, TOK), TOK)

    def part(piece, half):
        source = (k, v)[piece % 2]
        return source.at[:, pl.ds(pl.multiple_of((half * 2 + piece // 2) * D, D), D)]

    def shelf(slot, piece):
        return kv.at[slot, piece]

    local = [pltpu.make_async_copy(part(p, core), kv.at[4, p, mine, :], pair_l.at[p]) for p in range(4)]
    loads = [
        pltpu.make_async_copy(do, d_v, load_s.at[0]),
        pltpu.make_async_copy(o, o_v, load_s.at[1]),
        pltpu.make_async_copy(do.at[:, here], dov.at[mine, :], load_s.at[2]),
        pltpu.make_async_copy(q.at[:, here], qv.at[mine, :], load_s.at[3]),
    ]
    for copy in local + loads:
        copy.start()
    actin[...] = jnp.zeros_like(actin)
    actin[0:2, 0:WIN] = act[...]
    enter(place)

    pair = [remote(part(p, other), kv.at[4, p, mine, :], pair_s.at[p], pair_r.at[p], sib) for p in range(4)]
    big = [remote(do.at[:, away], dov.at[mine, :], big_s.at[0], big_r.at[0], sib),
           remote(q.at[:, away], qv.at[mine, :], big_s.at[1], big_r.at[1], sib)]
    small = [remote(actin, actbuf, small_s.at[0], small_r.at[0], sib),
             remote(theirs, rows.at[core], small_s.at[1], small_r.at[1], sib)]
    for copy in pair + [small[0]] + big:
        copy.start()

    up = [remote(shelf(4, p), shelf(0, p), up_s.at[p], up_r.at[p], place.line(1)) for p in range(4)]
    own_line = [[remote(shelf(4, p), shelf(4 - s, p), line_s.at[s - 1, p], line_r.at[s - 1, p], place.later(s))
                 for p in range(4)] for s in (1, 2, 3)]
    prev_line = [[remote(shelf(0, p), shelf(4 - s, p), line_s.at[s - 1, p], line_r.at[s - 1, p], place.later(s))
                  for p in range(4)] for s in (1, 2, 3)]
    for p in range(4):
        local[p].wait()
        pair[p].wait()
        up[p].start()
        for s in (1, 3):
            @pl.when(x + s < 4)
            def _(s=s, p=p):
                own_line[s - 1][p].start()

    loads[0].wait()
    loads[1].wait()
    spread = jnp.where(lax.broadcasted_iota(I32, (8, 8 * D), 1) // D == lax.broadcasted_iota(I32, (8, 8 * D), 0),
                       1.0, 0.0).astype(BF16)
    for g in range(4):
        cols = slice(g * 8 * D, (g + 1) * 8 * D)
        product = d_v[:, cols].astype(F32) * o_v[:, cols].astype(F32)
        high = product.astype(BF16)
        low = (product - high.astype(F32)).astype(BF16)
        delta = dot(spread, high, NT) + dot(spread, low, NT)
        logs = lse[g * 8:(g + 1) * 8, :] * LOG2E

        @pl.when(core == g // 2)
        def _(delta=delta, logs=logs, g=g):
            rows[core, 0, g % 2] = logs
            rows[core, 1, g % 2] = delta

        @pl.when(core != g // 2)
        def _(delta=delta, logs=logs, g=g):
            theirs[0, g % 2] = logs
            theirs[1, g % 2] = delta

    small[1].start()

    seg_all = seg[...]
    seg_here = seg[pl.ds(chip * 4, 4), :]
    first = jnp.zeros((4, BLK), I32)
    for s in range(1, NSEG):
        first = jnp.where(seg_here == s, jnp.sum((seg_all < s).astype(I32)), first)
    small[0].wait()
    flags = [jnp.where(core == 0, actin[...], actbuf[...]), jnp.where(core == 0, actbuf[...], actin[...])]
    firsts[...] = jnp.full(firsts.shape, 2 ** 30, I32)
    for a in range(4):
        for d in range(WIN):
            flag = jnp.broadcast_to(flags[a // 2][a % 2:a % 2 + 1, d:d + 1], (1, BLK))
            firsts[a, d:d + 1, :] = jnp.where(flag > 0, first[a:a + 1, :], 2 ** 30)
    dq_sum[...] = jnp.zeros_like(dq_sum)

    key_at = lax.broadcasted_iota(I32, (BLK, BLK), 0)
    query_at = lax.broadcasted_iota(I32, (1, BLK), 1)

    def tile(slot, a, h, heads=(0, 1)):
        keys = pl.ds(pl.multiple_of(h * 2 * BLK, 2 * BLK), 2 * BLK)
        tokens = pl.ds(pl.multiple_of(a * BLK, BLK), BLK)
        lanes = pl.ds(pl.multiple_of(lax.rem(a, 2) * BLK, BLK), BLK)
        half = lax.div(a, 2)
        bias = []
        for b in range(2):
            rel = slot * 4 + h * 2 + b
            base = (chip * 4 - 16 + rel) * BLK
            low = firsts[a, pl.ds(jnp.maximum(16 + a - rel, 0), 1), :] - base
            high = (chip * 4 + a) * BLK - base + query_at
            bias.append(jnp.where((key_at >= low) & (key_at <= high), 0.0, LOWEST))
        bias = jnp.concatenate(bias, 0)
        for g in heads:
            key, value = kv[slot, 2 * g, keys, :], kv[slot, 2 * g + 1, keys, :]
            columns = [slice((g * 8 + j) * D, (g * 8 + j + 1) * D) for j in range(8)]
            query = jnp.concatenate([qv[tokens, c] for c in columns], 0)
            cotangent = jnp.concatenate([dov[tokens, c] for c in columns], 0)
            scores = dot(key, query, NT)
            grad_weights = dot(value, cotangent, NT)
            weights, grad_scores = [], []
            for j in range(8):
                lane = slice(j * BLK, (j + 1) * BLK)
                log_row = rows[half, 0, g, j:j + 1, lanes]
                delta_row = rows[half, 1, g, j:j + 1, lanes]
                weight = jnp.exp2(scores[:, lane] * (FACTOR * LOG2E) - log_row + bias)
                weights.append(weight.astype(BF16))
                grad_scores.append((weight * (grad_weights[:, lane] - delta_row)).astype(BF16))
            weights = jnp.concatenate(weights, 1)
            grad_scores = jnp.concatenate(grad_scores, 1)
            kv_sum[2 * g, keys, :] += dot(grad_scores, query, NN)
            kv_sum[2 * g + 1, keys, :] += dot(weights, cotangent, NN)
            dq_sum[a, g] += dot(key, grad_scores, TN)

    def phase(slot, steps, pairs, after=None, heads=(0, 1)):
        for g in heads:
            kv_sum[2 * g:2 * g + 2] = jnp.zeros((2, CHIP, D), F32)

        def step(i, carry):
            for a, h in pairs(i):
                tile(slot, a, h, heads)
            if after is not None:
                after(i)
            return carry

        lax.fori_loop(0, steps, step, 0)

    back = [[remote(parts.at[s - 1, p], got.at[s - 1, p], back_s.at[s - 1, p], back_r.at[s - 1, p], place.later(4 - s))
             for p in range(4)] for s in (1, 2, 3)]

    def send_two():
        for p in range(4):
            @pl.when(x < 2)
            def _(p=p):
                own_line[1][p].start()

            @pl.when(x >= 2)
            def _(p=p):
                prev_line[1][p].start()

    def full_phase(s):
        for p in range(4):
            prev_line[s - 1][p].wait_recv()
        if s == 1:
            send_two()
        phase(4 - s, 4, lambda i: [(i, 0), (i, 1)])
        for p in range(4):
            parts[s - 1, p] = (kv_sum[p] * (FACTOR if p % 2 == 0 else 1.0)).astype(BF16)
            back[s - 1][p].start()

    def forward(p):
        remote(shelf(4, p), shelf(0, p), up_s.at[p], up_r.at[p], place.line(1)).wait_recv()
        for s in (1, 3):
            @pl.when(x + s >= 4)
            def _(s=s):
                remote(shelf(0, p), shelf(4 - s, p), line_s.at[s - 1, p], line_r.at[s - 1, p], place.later(s)).start()

    def own_pairs(i):
        i = lax.rem(i + core, 3)
        return [(jnp.where(i == 0, 0, i + 1), 0), (i + 1, jnp.where(i == 0, 0, 1))]

    def first_step(i):
        @pl.when(i == 0)
        def _():
            forward(0)
            forward(1)
            for copy in big + [small[1]]:
                copy.wait()

        @pl.when(i > 0)
        def _():
            forward(i + 1)

    loads[2].wait()
    loads[3].wait()
    phase(4, 3, own_pairs, first_step)
    for p in range(4):
        own_sum[p] = kv_sum[p] * (FACTOR if p % 2 == 0 else 1.0)
    def keep_far():
        for p in range(4):
            far[p] = (kv_sum[p] * (FACTOR if p % 2 == 0 else 1.0)).astype(BF16)

    phase(0, 2, lambda i: [(i, i), (2 * i, 1)])
    keep_far()
    full_phase(1)
    full_phase(3)
    for p in range(4):
        prev_line[1][p].wait_recv()
    down = [remote(relay.at[p], got.at[3, p], down_s.at[p], down_r.at[p], place.line(-1)) for p in range(4)]

    def pass_down(p):
        final[...] = far[p].astype(F32)
        for s in (1, 3, 2):
            @pl.when(x + s >= 4)
            def _(s=s):
                back[s - 1][p].wait_recv()
                final[...] += got[s - 1, p].astype(F32)
        relay[p] = final[...].astype(BF16)
        down[p].start()

    def early(i):
        @pl.when(i == 0)
        def _():
            pass_down(0)

    for g in range(2):
        phase(2, 2, lambda i: [(2 * i, 0), (2 * i, 1), (2 * i + 1, 0), (2 * i + 1, 1)],
              early if g == 1 else None, heads=(g,))
        for p in (2 * g, 2 * g + 1):
            parts[1, p] = (kv_sum[p] * (FACTOR if p % 2 == 0 else 1.0)).astype(BF16)
            back[1][p].start()

    def turn(i, carry):
        a, g = lax.div(i, 2), lax.rem(i, 2)
        tokens = pl.ds(pl.multiple_of(a * BLK, BLK), BLK)
        for j in range(8):
            block = dq_sum[a, g, :, j * BLK:(j + 1) * BLK].T * FACTOR
            dq[tokens, pl.ds(pl.multiple_of((g * 8 + j) * D, D), D)] = block.astype(BF16)
        return carry

    pass_down(1)
    lax.fori_loop(0, 8, turn, 0)
    send_q = remote(dq.at[others, :], gq.at[:, here], q_s.at[0], q_r.at[0], sib)
    send_q.start()
    keep_q = pltpu.make_async_copy(dq.at[mine, :], gq.at[:, here], load_s.at[4])
    keep_q.start()
    pass_down(2)
    pass_down(3)
    for p in range(4):
        for s in (1, 3, 2):
            @pl.when(x + s < 4)
            def _(s=s, p=p):
                back[s - 1][p].wait_recv()
                own_sum[p] += got[s - 1, p].astype(F32)
    finish, keep = [], []
    for p in range(4):
        down[p].wait_recv()
        far[p] = (own_sum[p] + got[3, p].astype(F32)).astype(BF16)
        target = (gk, gv)[p % 2].at[:, pl.ds(pl.multiple_of((core * 2 + p // 2) * D, D), D)]
        finish.append(remote(far.at[p, others, :], target, fin_s.at[p], fin_r.at[p], sib))
        keep.append(pltpu.make_async_copy(far.at[p, mine, :], target, out_s.at[p]))
        finish[p].start()
        keep[p].start()
    for p in range(4):
        keep[p].wait()
        finish[p].wait()
        up[p].wait_send()
        down[p].wait_send()
        for s in (1, 2, 3):
            prev_line[s - 1][p].wait_send()
            back[s - 1][p].wait_send()
    send_q.wait()
    keep_q.wait()


def body(queries, keys, values, fwd_out, log_sum, out_grad, seg_ids, active):
    anywhere = pl.BlockSpec(memory_space=pl.ANY)
    vmem = pl.BlockSpec(memory_space=pltpu.VMEM)
    dma = pltpu.SemaphoreType.DMA
    seg = seg_ids.reshape(BLK, BLK)
    return tuple(pl.pallas_call(
        fused_kernel,
        out_shape=[
            jax.ShapeDtypeStruct((TOK, 2 * HALF), BF16),
            jax.ShapeDtypeStruct((TOK, 4 * D), BF16),
            jax.ShapeDtypeStruct((TOK, 4 * D), BF16),
        ],
        in_specs=[anywhere, anywhere, anywhere, anywhere, vmem, anywhere, vmem, vmem],
        out_specs=[anywhere] * 3,
        scratch_shapes=[
            pltpu.VMEM((5, 4, CHIP, D), BF16),
            pltpu.VMEM((CHIP, HALF), BF16),
            pltpu.VMEM((CHIP, HALF), BF16),
            pltpu.VMEM((TOK, 2 * HALF), BF16),
            pltpu.VMEM((TOK, 2 * HALF), BF16),
            pltpu.VMEM((2, 2, 2, 8, TOK), F32),
            pltpu.VMEM((2, 2, 8, TOK), F32),
            pltpu.VMEM((8, BLK), I32),
            pltpu.VMEM((8, BLK), I32),
            pltpu.VMEM((4, 24, BLK), I32),
            pltpu.VMEM((4, 2, D, 8 * BLK), F32),
            pltpu.VMEM((4, CHIP, D), F32),
            pltpu.VMEM((4, CHIP, D), F32),
            pltpu.VMEM((3, 4, CHIP, D), BF16),
            pltpu.VMEM((4, CHIP, D), BF16),
            pltpu.VMEM((4, 4, CHIP, D), BF16),
            pltpu.VMEM((4, CHIP, D), BF16),
            pltpu.VMEM((CHIP, D), F32),
            pltpu.VMEM((CHIP, HALF), BF16),
            dma((5,)), dma((4,)), dma((4,)), dma((4,)), dma((4,)), dma((4,)), dma((3, 4)), dma((3, 4)),
            dma((2,)), dma((2,)), dma((2,)), dma((2,)),
            dma((3, 4)), dma((3, 4)), dma((4,)), dma((4,)), dma((4,)), dma((4,)), dma((4,)), dma((1,)), dma((1,)),
        ],
        compiler_params=pltpu.CompilerParams(
            collective_id=0, has_side_effects=True, vmem_limit_bytes=63 * 2 ** 20),
        cost_estimate=pl.CostEstimate(flops=25 * 10 ** 9, bytes_accessed=12 * 2 ** 20, transcendentals=0),
        name="fused",
    )(queries, keys, values, fwd_out, log_sum, out_grad, seg, active))


def solution(mesh):
    placed = (
        P("ctx", "kvh"), P("ctx", "kvh"), P("ctx", "kvh"), P("ctx", "kvh"),
        P("kvh", "ctx"), P("ctx", "kvh"), P(), P("ctx", None),
    )
    return jax.shard_map(
        body, mesh=mesh, in_specs=placed,
        out_specs=(P("ctx", "kvh"), P("ctx", "kvh"), P("ctx", "kvh")),
        check_vma=False,
    )
```
